32 devices in a mesh: groups: 2 (over x), mp: 16 (over z, y, core).
Axes of the slice: x: 2, y: 2, z: 4, core: 2. Of those that a mesh axis runs over, the one named last changes fastest.
Arguments:
- features: bfloat16 [32, 256, 128, 128], P(None, ('groups', 'mp')), parts along dimension 1, may hold values from -6 to 6
- cotangent: bfloat16 [32, 256, 128, 128], P(None, ('groups', 'mp')), parts along dimension 1, may hold values from -9 to 9
- spectral_weight: float32 [256, 2, 16, 32, 32], P('mp'), may hold values from -9 to 9
- pointwise_weight: bfloat16 [32, 32], replicated, may hold values from -1 to 1
- biases: float32 [32], replicated, may hold values from -3 to 3
Outputs:
- features_grad: bfloat16 [32, 256, 128, 128], P(None, ('groups', 'mp')), parts along dimension 1
- spectral_grad: float32 [512, 2, 16, 32, 32], P(('groups', 'mp')), parts along dimension 0
- pointwise_grad: float32 [64, 32], P('groups'), parts along dimension 0
- biases_grad: float32 [64], P('groups'), parts along dimension 0
The draws below stay inside these ranges and needn't reach their ends.
There are 2 independent parts, one for each index of `groups`. The reference program is written for one: setup_inputs(seed, part) draws one part's arguments, and reference() takes and returns one part's arrays. A program takes and returns all parts, laid end to end along the dimension named above; an argument that names none is the same for every part. Nothing has to cross between parts.
All inputs are finite; a program needn't handle non-finite values.
Results may differ from the reference program's by a relative error of at most 0.007.
Values sent between devices are 32-bit elements; how exact they have to be, the bound alone decides.
A program may use at most 128 MiB of HBM per device.

```python
import math
import jax
import jax.numpy as jnp
from jax import lax

C = 32
NX = 128
NY = 128
NZ = 128
KX = 16
KY = 16
KZ = 16
PAIRS = 256


def draw_cotangent(key, part):
    ramp = 0.5 + jnp.arange(NX, dtype=jnp.float32) * (1.0 / (NX - 1))
    base = jnp.clip(jax.random.normal(key, (C, NX, NY, NZ), jnp.float32), -5.5, 5.5)
    return (base * ramp[None, :, None, None]).astype(jnp.bfloat16)


def shard_levels(key, shape, pieces, smallest, largest):
    loudness = 1.0
    for dim, shards_of in pieces:
        steps = jax.random.uniform(jax.random.fold_in(jax.random.fold_in(key, 6), dim), (shards_of,), jnp.float32, smallest / len(pieces), largest / len(pieces))
        loudness = loudness * jnp.repeat(jnp.exp(steps), shape[dim] // shards_of).reshape((-1,) + (1,) * (len(shape) - 1 - dim))
    return loudness


def gaussian(key, dims, deviation, reach, cuts=(), kind=jnp.bfloat16):
    result = jax.random.normal(key, dims, jnp.float32) * deviation
    if len(cuts) > 0:
        result = shard_levels(key, dims, cuts, -0.22, 0.18) * result
    return jnp.clip(result, min=-reach, max=reach).astype(kind)


def setup_inputs(seed: int = 0, part: int = 0) -> dict:
    seeds = jax.random.split(jax.random.key(seed), 6)
    own_keys = jax.random.split(jax.random.fold_in(seeds[5], part), 6)
    return {
        "features": gaussian(own_keys[0], (C, NX, NY, NZ), 1.0, 6.0, ((1, 16),)),
        "cotangent": draw_cotangent(jax.random.fold_in(jax.random.fold_in(seeds[5], part), 71), part),
        "spectral_weight": gaussian(seeds[2], (PAIRS, 2, KX, C, C), 1.5, 9.0, ((0, 16),), jnp.float32),
        "pointwise_weight": gaussian(seeds[3], (C, C), C ** -0.5, 1.0),
        "biases": gaussian(seeds[4], (C,), 0.5, 3.0, (), jnp.float32),
    }


precise = lax.Precision.HIGHEST

def axis_tables(length, mode_count, signed):
    freqs = jnp.arange(mode_count, dtype=jnp.int32) - (mode_count // 2 if signed else 0)
    spots = jnp.arange(length, dtype=jnp.int32)
    phases = (spots[:, None] * freqs[None, :] % length).astype(jnp.float32) * (2.0 * math.pi / length)
    return (jnp.cos(phases), jnp.sin(phases))

def spectrum_plane(data, z_cos, z_sin, y_cos, y_sin, z_scale):
    hold = data.astype(jnp.float32)
    z_real = jnp.einsum('cxyz,zk->kcxy', hold, z_cos, precision=precise) * z_scale[:, None, None, None]
    z_imag = -jnp.einsum('cxyz,zk->kcxy', hold, z_sin, precision=precise) * z_scale[:, None, None, None]
    y_real = jnp.einsum('kcxy,yj->jkcx', z_real, y_cos, precision=precise) + jnp.einsum('kcxy,yj->jkcx', z_imag, y_sin, precision=precise)
    y_imag = jnp.einsum('kcxy,yj->jkcx', z_imag, y_cos, precision=precise) - jnp.einsum('kcxy,yj->jkcx', z_real, y_sin, precision=precise)
    stacked = jnp.stack([y_real, y_imag], axis=2)
    return stacked.reshape(KY * KZ, 2, stacked.shape[3], stacked.shape[4])

def spectrum_lines(part, x_cos, x_sin):
    a_real = part[:, 0]
    a_imag = part[:, 1]
    v_real = jnp.einsum('pcx,xk->pck', a_real, x_cos, precision=precise) + jnp.einsum('pcx,xk->pck', a_imag, x_sin, precision=precise)
    v_imag = jnp.einsum('pcx,xk->pck', a_imag, x_cos, precision=precise) - jnp.einsum('pcx,xk->pck', a_real, x_sin, precision=precise)
    return jnp.stack([v_real, v_imag], axis=1)

def space_lines(spec, x_cos, x_sin):
    u_real = spec[:, 0]
    u_imag = spec[:, 1]
    b_real = jnp.einsum('pck,xk->pcx', u_real, x_cos, precision=precise) - jnp.einsum('pck,xk->pcx', u_imag, x_sin, precision=precise)
    b_imag = jnp.einsum('pck,xk->pcx', u_imag, x_cos, precision=precise) + jnp.einsum('pck,xk->pcx', u_real, x_sin, precision=precise)
    return jnp.stack([b_real, b_imag], axis=1)

def space_plane(stacked, y_cos, y_sin, z_cos, z_sin):
    grid = stacked.reshape(KY, KZ, 2, stacked.shape[2], stacked.shape[3])
    q_real = grid[:, :, 0]
    q_imag = grid[:, :, 1]
    b_real = jnp.einsum('jkcx,yj->kcxy', q_real, y_cos, precision=precise) - jnp.einsum('jkcx,yj->kcxy', q_imag, y_sin, precision=precise)
    b_imag = jnp.einsum('jkcx,yj->kcxy', q_imag, y_cos, precision=precise) + jnp.einsum('jkcx,yj->kcxy', q_real, y_sin, precision=precise)
    return jnp.einsum('kcxy,zk->cxyz', b_real, z_cos, precision=precise) - jnp.einsum('kcxy,zk->cxyz', b_imag, z_sin, precision=precise)

def modes_product(spec, weight):
    v_real, v_imag = (spec[:, 0], spec[:, 1])
    r_real, r_imag = (weight[:, 0], weight[:, 1])
    u_real = jnp.einsum('pck,pkco->pok', v_real, r_real, precision=precise) - jnp.einsum('pck,pkco->pok', v_imag, r_imag, precision=precise)
    u_imag = jnp.einsum('pck,pkco->pok', v_real, r_imag, precision=precise) + jnp.einsum('pck,pkco->pok', v_imag, r_real, precision=precise)
    return jnp.stack([u_real, u_imag], axis=1)

def modes_adjoint(dspec, weight):
    d_real, d_imag = (dspec[:, 0], dspec[:, 1])
    r_real, r_imag = (weight[:, 0], weight[:, 1])
    g_real = jnp.einsum('pok,pkco->pck', d_real, r_real, precision=precise) + jnp.einsum('pok,pkco->pck', d_imag, r_imag, precision=precise)
    g_imag = jnp.einsum('pok,pkco->pck', d_imag, r_real, precision=precise) - jnp.einsum('pok,pkco->pck', d_real, r_imag, precision=precise)
    return jnp.stack([g_real, g_imag], axis=1)

def modes_gradient(spec, dspec):
    v_real, v_imag = (spec[:, 0], spec[:, 1])
    d_real, d_imag = (dspec[:, 0], dspec[:, 1])
    w_real = jnp.einsum('pck,pok->pkco', v_real, d_real, precision=precise) + jnp.einsum('pck,pok->pkco', v_imag, d_imag, precision=precise)
    w_imag = jnp.einsum('pck,pok->pkco', v_real, d_imag, precision=precise) - jnp.einsum('pck,pok->pkco', v_imag, d_real, precision=precise)
    return jnp.stack([w_real, w_imag], axis=1)

def reference(features, cotangent, spectral_weight, pointwise_weight, biases):
    z_cos, z_sin = axis_tables(NZ, KZ, False)
    z_cos = lax.optimization_barrier(z_cos.astype(jnp.bfloat16)).astype(jnp.float32)
    z_sin = lax.optimization_barrier(z_sin.astype(jnp.bfloat16)).astype(jnp.float32)
    y_cos, y_sin = axis_tables(NY, KY, True)
    x_cos, x_sin = axis_tables(NX, KX, True)
    z_cos_full, z_sin_full = axis_tables(NZ, KZ, False)
    z_weight = jnp.where(jnp.arange(KZ) == 0, 1.0, 2.0).astype(jnp.float32) / float(NX * NY * NZ)
    unit_weight = jnp.ones((KZ,), jnp.float32)
    spec = spectrum_lines(spectrum_plane(features, z_cos, z_sin, y_cos, y_sin, unit_weight), x_cos, x_sin)
    mixed = modes_product(spec, spectral_weight)
    spectral = space_plane(space_lines(mixed, x_cos, x_sin), y_cos, y_sin, z_cos_full * z_weight[None, :], z_sin_full * z_weight[None, :])
    feats = features.astype(jnp.float32)
    mixer = pointwise_weight.astype(jnp.float32)
    preact = spectral + jnp.einsum('oc,cxyz->oxyz', mixer, feats, precision=precise) + biases[:, None, None, None]
    _, pullback = jax.vjp(jax.nn.gelu, preact)
    pre_grad = pullback(cotangent.astype(jnp.float32))[0].astype(jnp.bfloat16)
    dspec = spectrum_lines(spectrum_plane(pre_grad, z_cos, z_sin, y_cos, y_sin, z_weight), x_cos, x_sin)
    spectral_grad = modes_gradient(spec, dspec)
    dmixed = modes_adjoint(dspec, spectral_weight)
    grads_f = pre_grad.astype(jnp.float32)
    back = space_plane(space_lines(dmixed, x_cos, x_sin), y_cos, y_sin, z_cos_full, z_sin_full)
    features_grad = (back + jnp.einsum('oc,oxyz->cxyz', mixer, grads_f, precision=precise)).astype(jnp.bfloat16)
    factor = float(NX * NY * NZ) ** (-0.5)
    pointwise_grad = jnp.einsum('oxyz,cxyz->oc', grads_f, feats, precision=precise) * factor
    biases_grad = lax.optimization_barrier(jnp.sum(grads_f, axis=(1, 2, 3))) * factor
    return (features_grad, spectral_grad, pointwise_grad, biases_grad)
```

```python
import functools
import math

import jax
import jax.numpy as jnp
import ml_dtypes
import numpy as np
from jax import lax
from jax.experimental import pallas as pl
from jax.experimental.pallas import tpu as pltpu
from jax.sharding import PartitionSpec as P

C = 32
NX = 128
NY = 128
NZ = 128
KX = 16
KY = 16
KZ = 16
SCALE = 1.0 / (NX * NY * NZ)
OCT = 8
BF = jnp.bfloat16
F32 = jnp.float32
precise = lax.Precision.HIGHEST
VMEM = pl.BlockSpec(memory_space=pltpu.VMEM)


def trig(length, mode_count, signed):
    freqs = np.arange(mode_count) - (mode_count // 2 if signed else 0)
    spots = np.arange(length)
    phases = (spots[:, None] * freqs[None, :] % length) * (2.0 * math.pi / length)
    return np.cos(phases), np.sin(phases)


def low(table):
    return np.asarray(table, np.float32).astype(ml_dtypes.bfloat16)


def tables(rows):
    zc, zs = trig(NZ, KZ, False)
    yc, ys = trig(NY, KY, True)
    xc, xs = trig(NX, KX, True)
    wz = np.where(np.arange(KZ) == 0, 1.0, 2.0) * SCALE
    eye = np.eye(rows)
    fy = np.einsum("syj,xw->sjxwy", np.stack([yc, ys]), eye).reshape(2 * KY * rows, rows * NY)
    gy = np.einsum("syj,xw->xysjw", np.stack([yc, -ys]), eye).reshape(rows * NY, 2 * KY * rows)
    zc_low = low(zc).astype(np.float64)
    zs_low = low(zs).astype(np.float64)
    oct_eye = np.eye(OCT)
    block = np.stack([np.stack([zc_low, -zs_low]), np.stack([-zs_low, -zc_low])])
    fz = np.einsum("srzk,ab->aszrbk", block, oct_eye).reshape(OCT * 2 * NZ, 2 * OCT * KZ)
    fz_w = (fz.reshape(-1, KZ) * wz).reshape(fz.shape)
    back = np.stack([np.stack([zc, zs]), np.stack([-zs, zc])])
    gz = np.einsum("rqzk,ab->rakbqz", back, oct_eye).reshape(2 * OCT * KZ, OCT * 2 * NZ)
    gz_w = (np.einsum("rqzk,ab,k->rakbqz", back, oct_eye, wz)).reshape(gz.shape)
    fx = np.concatenate([xc.T, xs.T], 0).astype(np.float32)
    gx = np.concatenate([xc, xs], 0).astype(np.float32)
    return low(fy), low(gy), low(fz), low(fz_w), low(gz), low(gz_w), fx, gx


def dot(a, b):
    return jnp.dot(a, b, preferred_element_type=F32)


def plane_forward(src, fy, fz, out, rows):
    lines = KY * rows

    @pl.loop(0, C // OCT)
    def _(g):
        parts = []
        for q in range(0, OCT, 2):
            pair = jnp.concatenate([src[g * OCT + q], src[g * OCT + q + 1]], axis=1)
            both = dot(fy[...], pair).astype(BF)
            for h in range(2):
                piece = both[:, h * NZ : (h + 1) * NZ]
                parts += [piece[:lines], piece[lines:]]
        res = dot(jnp.concatenate(parts, axis=1), fz[...])
        half = OCT * KZ
        for r in range(2):
            at = pl.multiple_of(r * C * KZ + g * half, 128)
            out[:, pl.ds(at, half)] = res[:, r * half : (r + 1) * half]


def plane_back(src, gz, gy, out, rows):
    @pl.loop(0, C // OCT)
    def _(g):
        half = OCT * KZ
        lhs = jnp.concatenate(
            [src[:, pl.ds(pl.multiple_of(r * C * KZ + g * half, 128), half)] for r in range(2)],
            axis=1,
        ).astype(BF)
        u = dot(lhs, gz[...]).astype(BF)
        for q in range(0, OCT, 2):
            cols = []
            for h in range(2):
                o = q + h
                cols.append(
                    jnp.concatenate(
                        [u[:, (2 * o + r) * NZ : (2 * o + r + 1) * NZ] for r in range(2)], axis=0
                    )
                )
            res = dot(gy[...], jnp.concatenate(cols, axis=1))
            out[g * OCT + q] = res[:, :NZ]
            out[g * OCT + q + 1] = res[:, NZ:]


def forward_kernel(rows, feat, fy, fz, out):
    plane_forward(feat, fy, fz, out, rows)


TILE = 16


def tile_of(ref, t):
    at = pl.multiple_of(t * TILE, TILE)
    return ref[:, pl.ds(at, TILE), :].reshape(C * TILE, NZ)


def middle_kernel(rows, feat, cot, modes, kron, bias, gz, gy, fy, fz, pg, part, pw, bsum, field, acc, bacc):
    plane_back(modes, gz, gy, field, rows)
    acc[...] = jnp.zeros_like(acc)
    bacc[...] = jnp.zeros_like(bacc)

    @pl.loop(0, rows * NY // (2 * TILE))
    def _(s):
        fs = [tile_of(feat, 2 * s + h) for h in range(2)]
        f = jnp.concatenate(fs, axis=1)
        mix = dot(kron[...], f)
        gs = []
        for h in range(2):
            t = 2 * s + h
            x = mix[:, h * NZ : (h + 1) * NZ] + tile_of(field, t) + bias[...]
            x2 = x * x
            a = math.sqrt(2.0 / math.pi)
            th = jnp.tanh(x * (a + (a * 0.044715) * x2))
            d = 0.5 * (1.0 + th) + (0.5 * x) * (1.0 - th * th) * (a + (3.0 * a * 0.044715) * x2)
            g = (tile_of(cot, t).astype(F32) * d).astype(BF)
            at = pl.multiple_of(t * TILE, TILE)
            pg[:, pl.ds(at, TILE), :] = g.reshape(C, TILE, NZ)
            bacc[...] += g.astype(F32)
            gs.append(g)
        g = jnp.concatenate(gs, axis=1)
        acc[...] += lax.dot_general(g, f, (((1,), (1,)), ((), ())), preferred_element_type=F32)

    n = C * TILE
    ri = lax.broadcasted_iota(jnp.int32, (n, n), 0)
    ci = lax.broadcasted_iota(jnp.int32, (n, n), 1)
    masked = jnp.where(ri % TILE == ci % TILE, acc[...], 0.0)
    rows_sum = jnp.sum(masked.reshape(C, TILE, n), axis=1)
    fold = jnp.where(
        lax.broadcasted_iota(jnp.int32, (n, C), 0) // TILE
        == lax.broadcasted_iota(jnp.int32, (n, C), 1),
        1.0,
        0.0,
    ).astype(F32)
    pw[...] = jnp.dot(rows_sum, fold, precision=precise, preferred_element_type=F32)
    bsum[...] = jnp.sum(bacc[...].reshape(C, TILE, NZ), axis=1)
    plane_forward(pg, fy, fz, part, rows)


def last_kernel(rows, pg, modes, kron, gz, gy, out, field):
    plane_back(modes, gz, gy, field, rows)

    @pl.loop(0, rows * NY // (2 * TILE))
    def _(s):
        f = jnp.concatenate([tile_of(pg, 2 * s + h) for h in range(2)], axis=1)
        mix = dot(kron[...], f)
        for h in range(2):
            t = 2 * s + h
            r = (mix[:, h * NZ : (h + 1) * NZ] + tile_of(field, t)).astype(BF)
            at = pl.multiple_of(t * TILE, TILE)
            out[:, pl.ds(at, TILE), :] = r.reshape(C, TILE, NZ)


def exchange_kernel(n, src, dst, send, recv, own):
    me = lax.axis_index("mp")
    barrier = pltpu.get_barrier_semaphore()

    @pl.loop(1, n)
    def _(s):
        pl.semaphore_signal(
            barrier, inc=1, device_id={"mp": lax.rem(me + s, n)}, device_id_type=pl.DeviceIdType.MESH
        )

    pl.semaphore_wait(barrier, n - 1)

    def copy(peer):
        return pltpu.make_async_remote_copy(
            src_ref=src.at[peer],
            dst_ref=dst.at[me],
            send_sem=send.at[peer],
            recv_sem=recv.at[me],
            device_id={"mp": peer},
            device_id_type=pl.DeviceIdType.MESH,
        )

    def arrival(peer):
        return pltpu.make_async_remote_copy(
            src_ref=src.at[peer],
            dst_ref=dst.at[peer],
            send_sem=send.at[peer],
            recv_sem=recv.at[peer],
            device_id={"mp": peer},
            device_id_type=pl.DeviceIdType.MESH,
        )

    @pl.loop(1, n)
    def _(s):
        copy(lax.rem(me + s, n)).start()

    mine = pltpu.make_async_copy(src.at[me], dst.at[me], own)
    mine.start()
    mine.wait()

    @pl.loop(1, n)
    def _(s):
        peer = lax.rem(me + s, n)
        arrival(peer).wait_recv()
        copy(peer).wait_send()


def exchange(x, n, cid):
    return pl.pallas_call(
        functools.partial(exchange_kernel, n),
        out_shape=jax.ShapeDtypeStruct(x.shape, x.dtype),
        in_specs=[VMEM],
        out_specs=VMEM,
        scratch_shapes=[
            pltpu.SemaphoreType.DMA((n,)),
            pltpu.SemaphoreType.DMA((n,)),
            pltpu.SemaphoreType.DMA,
        ],
        compiler_params=pltpu.CompilerParams(
            collective_id=cid, has_side_effects=True, vmem_limit_bytes=16 << 20
        ),
        name=f"exchange{cid}",
    )(x)


def call(kernel, rows, outs, scratch, args, name):
    return pl.pallas_call(
        functools.partial(kernel, rows),
        out_shape=outs,
        in_specs=[VMEM] * len(args),
        out_specs=jax.tree.map(lambda _: VMEM, outs),
        scratch_shapes=scratch,
        compiler_params=pltpu.CompilerParams(vmem_limit_bytes=60 << 20),
        name=name,
    )(*args)


def to_owner(part, n, rows, cid):
    subs = n // KY
    if subs > 1:
        v = part.reshape(KY, rows, 2 * C, subs, KZ // subs)
        part = jnp.transpose(v, (0, 3, 1, 2, 4))
    blocks = part.reshape(n, rows, 2 * C * KZ // subs)
    return exchange(blocks, n, cid).reshape(NX, 2 * C * KZ // subs)


def to_plane(lines, n, rows, cid):
    subs = n // KY
    got = exchange(lines.reshape(n, rows, lines.shape[1]), n, cid)
    if subs > 1:
        v = got.reshape(KY, subs, rows, 2 * C, KZ // subs)
        got = jnp.transpose(v, (0, 2, 3, 1, 4))
    return got.reshape(KY * rows, 2 * C * KZ)


def lines_forward(g, fx):
    t = jnp.einsum("qx,xl->ql", fx, g, precision=precise).reshape(2, KX, 2, C, -1)
    real = t[0, :, 0] + t[1, :, 1]
    imag = t[0, :, 1] - t[1, :, 0]
    return jnp.transpose(real, (2, 0, 1)), jnp.transpose(imag, (2, 0, 1))


def lines_back(real, imag, gx):
    u = jnp.stack([real, imag])
    u = jnp.transpose(u, (2, 0, 3, 1)).reshape(KX, -1)
    b = jnp.einsum("qa,al->ql", gx, u, precision=precise).reshape(2, NX, 2, -1)
    return jnp.stack([b[0, :, 0] - b[1, :, 1], b[0, :, 1] + b[1, :, 0]], 1).reshape(NX, -1)


def shards(features, cotangent, spectral_weight, pointwise_weight, biases):
    n = lax.axis_size("mp")
    rows = NX // n
    fy, gy, fz, fz_w, gz, gz_w, fx, gx = [jnp.asarray(t) for t in tables(rows)]
    cells = rows * NY
    feat = features.reshape(C, cells, NZ)
    cot = cotangent.reshape(C, cells, NZ)
    eye = jnp.eye(TILE, dtype=BF)
    kron = jnp.kron(pointwise_weight, eye)
    kron_t = jnp.kron(pointwise_weight.T, eye)
    bias = jnp.repeat(biases, TILE)[:, None]
    spread = jax.ShapeDtypeStruct((KY * rows, 2 * C * KZ), F32)
    field = pltpu.VMEM((C, cells, NZ), F32)
    part = call(forward_kernel, rows, spread, [], (feat, fy, fz), "analysis")
    v_r, v_i = lines_forward(to_owner(part, n, rows, 1), fx)
    w_r, w_i = spectral_weight[:, 0], spectral_weight[:, 1]
    s_r, s_i = v_r[..., None], v_i[..., None]
    u_r = jnp.sum(s_r * w_r - s_i * w_i, axis=2)
    u_i = jnp.sum(s_r * w_i + s_i * w_r, axis=2)
    modes = to_plane(lines_back(u_r, u_i, gx), n, rows, 2)
    pg, dpart, pw, bsum = call(
        middle_kernel,
        rows,
        (
            jax.ShapeDtypeStruct((C, cells, NZ), BF),
            spread,
            jax.ShapeDtypeStruct((C, C), F32),
            jax.ShapeDtypeStruct((C, NZ), F32),
        ),
        [field, pltpu.VMEM((C * TILE, C * TILE), F32), pltpu.VMEM((C * TILE, NZ), F32)],
        (feat, cot, modes, kron, bias, gz_w, gy, fy, fz_w),
        "middle",
    )
    d_r, d_i = lines_forward(to_owner(dpart, n, rows, 3), fx)
    e_r, e_i = d_r[:, :, None, :], d_i[:, :, None, :]
    spectral_grad = jnp.stack([s_r * e_r + s_i * e_i, s_r * e_i - s_i * e_r], axis=1)
    m_r = jnp.sum(e_r * w_r + e_i * w_i, axis=3)
    m_i = jnp.sum(e_i * w_r - e_r * w_i, axis=3)
    back = to_plane(lines_back(m_r, m_i, gx), n, rows, 4)
    grad = call(
        last_kernel,
        rows,
        jax.ShapeDtypeStruct((C, cells, NZ), BF),
        [field],
        (pg, back, kron_t, gz, gy),
        "synthesis",
    )
    factor = float(NX * NY * NZ) ** (-0.5)
    sums = jnp.concatenate([pw, jnp.sum(bsum, axis=1)[:, None]], axis=1)
    total = jnp.sum(lax.all_gather(sums, "mp"), axis=0) * factor
    return (grad.reshape(features.shape), spectral_grad, total[:, :C], total[:, C])


def solution(mesh):
    return jax.shard_map(
        shards,
        mesh=mesh,
        in_specs=(
            P(None, ("groups", "mp"), None, None),
            P(None, ("groups", "mp"), None, None),
            P("mp", None, None, None, None),
            P(),
            P(),
        ),
        out_specs=(
            P(None, ("groups", "mp"), None, None),
            P(("groups", "mp"), None, None, None, None),
            P("groups", None),
            P("groups"),
        ),
        check_vma=False,
    )
```

```python
import functools
import math

import jax
import jax.numpy as jnp
import ml_dtypes
import numpy as np
from jax import lax
from jax.experimental import pallas as pl
from jax.experimental.pallas import tpu as pltpu
from jax.sharding import PartitionSpec as P

C = 32
NX = 128
NY = 128
NZ = 128
KX = 16
KY = 16
KZ = 16
SCALE = 1.0 / (NX * NY * NZ)
OCT = 8
GROUPS = C // OCT
GLANES = 2 * OCT * KZ
LANES = 128
SAVES = 4
BF = jnp.bfloat16
F32 = jnp.float32
precise = lax.Precision.HIGHEST
VMEM = pl.BlockSpec(memory_space=pltpu.VMEM)
HBM = pl.BlockSpec(memory_space=pl.ANY)


def trig(length, mode_count, signed):
    freqs = np.arange(mode_count) - (mode_count // 2 if signed else 0)
    spots = np.arange(length)
    phases = (spots[:, None] * freqs[None, :] % length) * (2.0 * math.pi / length)
    return np.cos(phases), np.sin(phases)


def low(table):
    return np.asarray(table, np.float32).astype(ml_dtypes.bfloat16)


def tables(rows):
    zc, zs = trig(NZ, KZ, False)
    yc, ys = trig(NY, KY, True)
    xc, xs = trig(NX, KX, True)
    wz = np.where(np.arange(KZ) == 0, 1.0, 2.0) * SCALE
    eye = np.eye(rows)
    fy = np.einsum("syj,xw->sjxwy", np.stack([yc, ys]), eye).reshape(2 * KY * rows, rows * NY)
    gy = np.einsum("syj,xw->xysjw", np.stack([yc, -ys]), eye).reshape(rows * NY, 2 * KY * rows)
    zc_low = low(zc).astype(np.float64)
    zs_low = low(zs).astype(np.float64)
    oct_eye = np.eye(OCT)
    block = np.stack([np.stack([zc_low, -zs_low]), np.stack([-zs_low, -zc_low])])
    fz = np.einsum("srzk,ab->aszrbk", block, oct_eye).reshape(OCT * 2 * NZ, 2 * OCT * KZ)
    fz_w = (fz.reshape(-1, KZ) * wz).reshape(fz.shape)
    back = np.stack([np.stack([zc, zs]), np.stack([-zs, zc])])
    gz = np.einsum("rqzk,ab->rakbqz", back, oct_eye).reshape(2 * OCT * KZ, OCT * 2 * NZ)
    gz_w = (np.einsum("rqzk,ab,k->rakbqz", back, oct_eye, wz)).reshape(gz.shape)
    fx = np.concatenate([xc.T, xs.T], 0).astype(np.float32)
    gx = np.concatenate([xc, xs], 0).astype(np.float32)
    return low(fy), low(gy), low(fz), low(fz_w), low(gz), low(gz_w), fx, gx


def dot(a, b):
    return jnp.dot(a, b, preferred_element_type=F32)


def forward_group(src, g, fy, fz, lines):
    parts = []
    for q in range(0, OCT, 2):
        pair = jnp.concatenate([src[g * OCT + q], src[g * OCT + q + 1]], axis=1)
        both = dot(fy[...], pair).astype(BF)
        for h in range(2):
            piece = both[:, h * NZ : (h + 1) * NZ]
            parts += [piece[:lines], piece[lines:]]
    return dot(jnp.concatenate(parts, axis=1), fz[...])


def plane_back(src, gz, gy, out):
    @pl.loop(0, GROUPS)
    def _(g):
        lhs = src[:, pl.ds(pl.multiple_of(g * GLANES, GLANES), GLANES)].astype(BF)
        u = dot(lhs, gz[...]).astype(BF)
        for q in range(0, OCT, 2):
            cols = []
            for h in range(2):
                o = q + h
                cols.append(
                    jnp.concatenate(
                        [u[:, (2 * o + r) * NZ : (2 * o + r + 1) * NZ] for r in range(2)], axis=0
                    )
                )
            res = dot(gy[...], jnp.concatenate(cols, axis=1))
            out[g * OCT + q] = res[:, :NZ]
            out[g * OCT + q + 1] = res[:, NZ:]


def plain_forward(src, fy, fz, out, lines):
    @pl.loop(0, GROUPS)
    def _(g):
        at = pl.multiple_of(g * GLANES, GLANES)
        out[:, pl.ds(at, GLANES)] = forward_group(src, g, fy, fz, lines)


def load_groups(hbm, buf, sems):
    copies = []
    for g in range(GROUPS):
        part = pl.ds(g * OCT, OCT)
        copies.append(pltpu.make_async_copy(hbm.at[part], buf.at[part], sems.at[g]))
        copies[-1].start()
    return copies


def greet(n):
    me = lax.axis_index("mp")

    @pl.loop(1, n)
    def _(s):
        pl.semaphore_signal(
            pltpu.get_barrier_semaphore(),
            inc=1,
            device_id={"mp": lax.rem(me + s, n)},
            device_id_type=pl.DeviceIdType.MESH,
        )


def remote(src, dst, send, recv, peer):
    return pltpu.make_async_remote_copy(
        src_ref=src,
        dst_ref=dst,
        send_sem=send,
        recv_sem=recv,
        device_id={"mp": peer},
        device_id_type=pl.DeviceIdType.MESH,
    )


def analysis_kernel(rows, n, feat_hbm, fy, fz, dst, feat, src, load, send, recv, own):
    me = lax.axis_index("mp")
    greet(n)
    loads = load_groups(feat_hbm, feat, load)
    mine = []
    wide = GLANES * GROUPS // 2
    for half in range(2):
        for g in range(half * GROUPS // 2, (half + 1) * GROUPS // 2):
            loads[g].wait()
            res = forward_group(feat, g, fy, fz, KY * rows)
            src[:, :, g * GLANES : (g + 1) * GLANES] = res.reshape(KY, rows, GLANES)
        lanes = pl.ds(half * wide, wide)
        if half == 0:
            pl.semaphore_wait(pltpu.get_barrier_semaphore(), n - 1)

        @pl.loop(1, n)
        def _(s):
            peer = lax.rem(me + s, n)
            remote(
                src.at[peer, :, lanes],
                dst.at[me, :, lanes],
                send.at[half, peer],
                recv.at[half, me],
                peer,
            ).start()

        mine.append(pltpu.make_async_copy(src.at[me, :, lanes], dst.at[me, :, lanes], own.at[half]))
        mine[-1].start()
    for half in range(2):
        lanes = pl.ds(half * wide, wide)
        mine[half].wait()

        @pl.loop(1, n)
        def _(s):
            peer = lax.rem(me + s, n)
            both = remote(
                src.at[peer, :, lanes],
                dst.at[peer, :, lanes],
                send.at[half, peer],
                recv.at[half, peer],
                peer,
            )
            both.wait_recv()
            both.wait_send()


def forward_kernel(rows, feat, fy, fz, out):
    plain_forward(feat, fy, fz, out, KY * rows)


TILE = 16
STEP = 4


def tile_of(ref, t):
    at = pl.multiple_of(t * TILE, TILE)
    return ref[:, pl.ds(at, TILE), :].reshape(C * TILE, NZ)


def put_tile(ref, t, value):
    at = pl.multiple_of(t * TILE, TILE)
    ref[:, pl.ds(at, TILE), :] = value.reshape(C, TILE, NZ)


def widen(weight):
    n = C * TILE
    row = lax.broadcasted_iota(jnp.int32, (n, C), 0) // TILE
    up = jnp.where(row == lax.broadcasted_iota(jnp.int32, (n, C), 1), 1.0, 0.0).astype(BF)
    left = dot(up, weight).astype(BF)
    full = lax.dot_general(left, up, (((1,), (1,)), ((), ())), preferred_element_type=F32)
    ri = lax.broadcasted_iota(jnp.int32, (n, n), 0)
    ci = lax.broadcasted_iota(jnp.int32, (n, n), 1)
    return jnp.where(ri % TILE == ci % TILE, full, 0.0).astype(BF)


def middle_kernel(
    rows, feat_hbm, cot_hbm, modes, weight, bias, gz, gy, fy, fz, pg_hbm, part, sums,
    field, acc, bacc, kron, feat, cot, pg, fsem, csem, psem,
):
    loads = load_groups(feat_hbm, feat, fsem) + load_groups(cot_hbm, cot, csem)
    kron[...] = widen(weight[...])
    acc[...] = jnp.zeros_like(acc)
    bacc[...] = jnp.zeros_like(bacc)
    plane_back(modes, gz, gy, field)
    for copy in loads:
        copy.wait()

    @pl.loop(0, rows * NY // (STEP * TILE))
    def _(s):
        f = jnp.concatenate([tile_of(feat, STEP * s + h) for h in range(STEP)], axis=1)
        mix = dot(kron[...], f)
        gs = []
        for h in range(STEP):
            t = STEP * s + h
            x = mix[:, h * NZ : (h + 1) * NZ] + tile_of(field, t) + bias[...]
            x2 = x * x
            a = math.sqrt(2.0 / math.pi)
            th = jnp.tanh(x * (a + (a * 0.044715) * x2))
            d = (0.5 + 0.5 * th) * (1.0 + (x * (1.0 - th)) * (a + (3.0 * a * 0.044715) * x2))
            g = (tile_of(cot, t).astype(F32) * d).astype(BF)
            put_tile(pg, t, g)
            gs.append(g)
        bacc[...] += sum(g.astype(F32) for g in gs)
        g = jnp.concatenate(gs, axis=1)
        acc[...] += lax.dot_general(g, f, (((1,), (1,)), ((), ())), preferred_element_type=F32)

    save = pltpu.make_async_copy(pg, pg_hbm, psem)
    save.start()
    n = C * TILE
    ri = lax.broadcasted_iota(jnp.int32, (n, n), 0)
    ci = lax.broadcasted_iota(jnp.int32, (n, n), 1)
    masked = jnp.where(ri % TILE == ci % TILE, acc[...], 0.0)
    rows_sum = jnp.sum(masked.reshape(C, TILE, n), axis=1)
    fold = jnp.where(
        lax.broadcasted_iota(jnp.int32, (n, LANES), 0) // TILE
        == lax.broadcasted_iota(jnp.int32, (n, LANES), 1),
        1.0,
        0.0,
    ).astype(F32)
    pw = jnp.dot(rows_sum, fold, precision=precise, preferred_element_type=F32)
    by_row = jnp.sum(bacc[...].reshape(C, TILE, NZ), axis=1)
    lane = lax.broadcasted_iota(jnp.int32, (C, LANES), 1)
    sums[...] = pw + jnp.where(lane == C, jnp.sum(by_row, axis=1, keepdims=True), 0.0)
    plain_forward(pg, fy, fz, part, KY * rows)
    save.wait()


def last_kernel(rows, pg_hbm, modes, weight, gz, gy, out_hbm, field, kron, pg, out, fsem, osem):
    loads = load_groups(pg_hbm, pg, fsem)
    kron[...] = widen(weight[...])
    plane_back(modes, gz, gy, field)
    for copy in loads:
        copy.wait()
    saves = []
    cells = rows * NY // SAVES
    for piece in range(SAVES):

        @pl.loop(0, cells // (STEP * TILE))
        def _(i):
            s = piece * (cells // (STEP * TILE)) + i
            f = jnp.concatenate([tile_of(pg, STEP * s + h) for h in range(STEP)], axis=1)
            mix = dot(kron[...], f)
            for h in range(STEP):
                t = STEP * s + h
                r = mix[:, h * NZ : (h + 1) * NZ] + tile_of(field, t)
                put_tile(out, t, r.astype(BF))

        at = pl.ds(piece * cells, cells)
        saves.append(pltpu.make_async_copy(out.at[:, at], out_hbm.at[:, at], osem.at[piece]))
        saves[-1].start()
    for copy in saves:
        copy.wait()


def exchange_kernel(n, arrays, *refs):
    srcs, dsts = refs[:arrays], refs[arrays : 2 * arrays]
    send, recv, own = refs[2 * arrays :]
    me = lax.axis_index("mp")
    greet(n)
    pl.semaphore_wait(pltpu.get_barrier_semaphore(), n - 1)

    @pl.loop(1, n)
    def _(s):
        peer = lax.rem(me + s, n)
        for i in range(arrays):
            remote(
                srcs[i].at[peer], dsts[i].at[me], send.at[i, peer], recv.at[i, me], peer
            ).start()

    for i in range(arrays):
        mine = pltpu.make_async_copy(srcs[i].at[me], dsts[i].at[me], own.at[i])
        mine.start()
        mine.wait()

    @pl.loop(1, n)
    def _(s):
        peer = lax.rem(me + s, n)
        for i in range(arrays):
            both = remote(
                srcs[i].at[peer], dsts[i].at[peer], send.at[i, peer], recv.at[i, peer], peer
            )
            both.wait_recv()
            both.wait_send()


def exchange(xs, n, cid):
    return pl.pallas_call(
        functools.partial(exchange_kernel, n, len(xs)),
        out_shape=[jax.ShapeDtypeStruct(x.shape, x.dtype) for x in xs],
        in_specs=[VMEM] * len(xs),
        out_specs=[VMEM] * len(xs),
        scratch_shapes=[
            pltpu.SemaphoreType.DMA((len(xs), n)),
            pltpu.SemaphoreType.DMA((len(xs), n)),
            pltpu.SemaphoreType.DMA((len(xs),)),
        ],
        compiler_params=pltpu.CompilerParams(
            collective_id=cid, has_side_effects=True, vmem_limit_bytes=16 << 20
        ),
        name=f"exchange{cid}",
    )(*xs)


def call(kernel, rows, outs, scratch, args, name, far=(), far_out=(), cid=None):
    outs = list(outs)
    params = {} if cid is None else {"collective_id": cid, "has_side_effects": True}
    return pl.pallas_call(
        functools.partial(kernel, rows),
        out_shape=outs,
        in_specs=[HBM if i in far else VMEM for i in range(len(args))],
        out_specs=[HBM if i in far_out else VMEM for i in range(len(outs))],
        scratch_shapes=scratch,
        compiler_params=pltpu.CompilerParams(vmem_limit_bytes=60 << 20, **params),
        name=name,
    )(*args)


def owner_blocks(part, n, rows):
    subs = n // KY
    if subs > 1:
        v = part.reshape(KY, rows, 2 * C, subs, KZ // subs)
        part = jnp.transpose(v, (0, 3, 1, 2, 4))
    return part.reshape(n, rows, 2 * C * KZ // subs)


def plane_blocks(got, n, rows):
    subs = n // KY
    if subs > 1:
        v = got.reshape(KY, subs, rows, 2 * C, KZ // subs)
        got = jnp.transpose(v, (0, 2, 3, 1, 4))
    return got.reshape(KY * rows, 2 * C * KZ)


def lines_forward(g, fx):
    g = g.reshape(NX, -1)
    t = jnp.einsum("qx,xl->ql", fx, g, precision=precise).reshape(2, KX, GROUPS, 2, OCT, -1)
    real = t[0, :, :, 0] + t[1, :, :, 1]
    imag = t[0, :, :, 1] - t[1, :, :, 0]
    real, imag = (jnp.transpose(v.reshape(KX, C, -1), (2, 0, 1)) for v in (real, imag))
    return real, imag


def lines_back(real, imag, gx, n, rows):
    u = jnp.stack([real, imag]).reshape(2, real.shape[0], KX, GROUPS, OCT)
    u = jnp.transpose(u, (2, 3, 0, 4, 1)).reshape(KX, -1)
    b = jnp.einsum("qa,al->ql", gx, u, precision=precise).reshape(2, NX, GROUPS, 2, -1)
    lines = jnp.stack([b[0, :, :, 0] - b[1, :, :, 1], b[0, :, :, 1] + b[1, :, :, 0]], 2)
    return lines.reshape(n, rows, -1)


def shards(features, cotangent, spectral_weight, pointwise_weight, biases):
    n = lax.axis_size("mp")
    rows = NX // n
    fy, gy, fz, fz_w, gz, gz_w, fx, gx = [jnp.asarray(t) for t in tables(rows)]
    cells = rows * NY
    feat = features.reshape(C, cells, NZ)
    cot = cotangent.reshape(C, cells, NZ)
    bias = jnp.repeat(biases, TILE)[:, None]
    spread = jax.ShapeDtypeStruct((KY * rows, 2 * C * KZ), F32)
    whole = jax.ShapeDtypeStruct((C, cells, NZ), BF)
    field = pltpu.VMEM((C, cells, NZ), F32)
    block = pltpu.VMEM((C, cells, NZ), BF)
    wide = C * TILE
    sems = pltpu.SemaphoreType.DMA((GROUPS,))
    if n == KY:
        blocks = jax.ShapeDtypeStruct((n, rows, 2 * C * KZ), F32)
        dma = pltpu.SemaphoreType.DMA
        got = call(
            lambda r, *refs: analysis_kernel(r, n, *refs),
            rows,
            [blocks],
            [block, pltpu.VMEM(blocks.shape, F32), sems, dma((2, n)), dma((2, n)), dma((2,))],
            (feat, fy, fz),
            "analysis",
            far=(0,),
            cid=1,
        )[0]
    else:
        part = call(forward_kernel, rows, [spread], [], (feat, fy, fz), "analysis")[0]
        got = exchange([owner_blocks(part, n, rows)], n, 1)[0]
    v_r, v_i = lines_forward(got, fx)
    w_r, w_i = spectral_weight[:, 0], spectral_weight[:, 1]
    s_r, s_i = v_r[..., None], v_i[..., None]
    u_r = jnp.sum(s_r * w_r - s_i * w_i, axis=2)
    u_i = jnp.sum(s_r * w_i + s_i * w_r, axis=2)
    modes = plane_blocks(exchange([lines_back(u_r, u_i, gx, n, rows)], n, 2)[0], n, rows)
    pg, dpart, sums = call(
        middle_kernel,
        rows,
        [whole, spread, jax.ShapeDtypeStruct((C, LANES), F32)],
        [
            field,
            pltpu.VMEM((wide, wide), F32),
            pltpu.VMEM((wide, NZ), F32),
            pltpu.VMEM((wide, wide), BF),
            block,
            block,
            block,
            sems,
            sems,
            pltpu.SemaphoreType.DMA,
        ],
        (feat, cot, modes, pointwise_weight, bias, gz_w, gy, fy, fz_w),
        "middle",
        far=(0, 1),
        far_out=(0,),
    )
    got, got_sums = exchange(
        [owner_blocks(dpart, n, rows), sums.reshape(n, C // n, LANES)], n, 3
    )
    d_r, d_i = lines_forward(got, fx)
    e_r, e_i = d_r[:, :, None, :], d_i[:, :, None, :]
    m_r = jnp.sum(e_r * w_r + e_i * w_i, axis=3)
    m_i = jnp.sum(e_i * w_r - e_r * w_i, axis=3)
    mine = jnp.broadcast_to(jnp.sum(got_sums, axis=0), (n, C // n, LANES))
    back, total = exchange([lines_back(m_r, m_i, gx, n, rows), mine], n, 4)
    spectral_grad = jnp.stack([s_r * e_r + s_i * e_i, s_r * e_i - s_i * e_r], axis=1)
    grad = call(
        last_kernel,
        rows,
        [whole],
        [field, pltpu.VMEM((wide, wide), BF), block, block, sems, pltpu.SemaphoreType.DMA((SAVES,))],
        (pg, plane_blocks(back, n, rows), pointwise_weight.T, gz, gy),
        "synthesis",
        far=(0,),
        far_out=(0,),
    )[0]
    factor = float(NX * NY * NZ) ** (-0.5)
    total = total.reshape(C, LANES) * factor
    return (grad.reshape(features.shape), spectral_grad, total[:, :C], total[:, C])


def solution(mesh):
    return jax.shard_map(
        shards,
        mesh=mesh,
        in_specs=(
            P(None, ("groups", "mp"), None, None),
            P(None, ("groups", "mp"), None, None),
            P("mp", None, None, None, None),
            P(),
            P(),
        ),
        out_specs=(
            P(None, ("groups", "mp"), None, None),
            P(("groups", "mp"), None, None, None, None),
            P("groups", None),
            P("groups"),
        ),
        check_vma=False,
    )
```

```python
import functools
import math

import jax
import jax.numpy as jnp
import ml_dtypes
import numpy as np
from jax import lax
from jax.experimental import pallas as pl
from jax.experimental.pallas import tpu as pltpu
from jax.sharding import PartitionSpec as P

C = 32
NX = 128
NY = 128
NZ = 128
KX = 16
KY = 16
KZ = 16
SCALE = 1.0 / (NX * NY * NZ)
OCT = 8
GROUPS = C // OCT
GLANES = 2 * OCT * KZ
LANES = 128
SAVES = 4
BF = jnp.bfloat16
F32 = jnp.float32
precise = lax.Precision.HIGHEST
VMEM = pl.BlockSpec(memory_space=pltpu.VMEM)
HBM = pl.BlockSpec(memory_space=pl.ANY)


def trig(length, mode_count, signed):
    freqs = np.arange(mode_count) - (mode_count // 2 if signed else 0)
    spots = np.arange(length)
    phases = (spots[:, None] * freqs[None, :] % length) * (2.0 * math.pi / length)
    return np.cos(phases), np.sin(phases)


def low(table):
    return np.asarray(table, np.float32).astype(ml_dtypes.bfloat16)


def tables(rows):
    zc, zs = trig(NZ, KZ, False)
    yc, ys = trig(NY, KY, True)
    xc, xs = trig(NX, KX, True)
    wz = np.where(np.arange(KZ) == 0, 1.0, 2.0) * SCALE
    eye = np.eye(rows)
    fy = np.einsum("syj,xw->sjxwy", np.stack([yc, ys]), eye).reshape(2 * KY * rows, rows * NY)
    gy = np.einsum("syj,xw->xysjw", np.stack([yc, -ys]), eye).reshape(rows * NY, 2 * KY * rows)
    zc_low = low(zc).astype(np.float64)
    zs_low = low(zs).astype(np.float64)
    oct_eye = np.eye(OCT)
    block = np.stack([np.stack([zc_low, -zs_low]), np.stack([-zs_low, -zc_low])])
    fz = np.einsum("srzk,ab->aszrbk", block, oct_eye).reshape(OCT * 2 * NZ, 2 * OCT * KZ)
    fz_w = (fz.reshape(-1, KZ) * wz).reshape(fz.shape)
    back = np.stack([np.stack([zc, zs]), np.stack([-zs, zc])])
    gz = np.einsum("rqzk,ab->rakbqz", back, oct_eye).reshape(2 * OCT * KZ, OCT * 2 * NZ)
    gz_w = (np.einsum("rqzk,ab,k->rakbqz", back, oct_eye, wz)).reshape(gz.shape)
    fx = np.concatenate([xc.T, xs.T], 0).astype(np.float32)
    gx = np.concatenate([xc, xs], 0).astype(np.float32)
    fx2 = np.block([[xc.T, xs.T], [-xs.T, xc.T]]).astype(np.float32)
    gx2 = np.block([[xc, -xs], [xs, xc]]).astype(np.float32)
    return low(fy), low(gy), low(fz), low(fz_w), low(gz), low(gz_w), fx, gx, fx2, gx2


def dot(a, b):
    return jnp.dot(a, b, preferred_element_type=F32)


def forward_group(src, g, fy, fz, lines):
    parts = []
    for q in range(0, OCT, 2):
        pair = jnp.concatenate([src[g * OCT + q], src[g * OCT + q + 1]], axis=1)
        both = dot(fy[...], pair).astype(BF)
        for h in range(2):
            piece = both[:, h * NZ : (h + 1) * NZ]
            parts += [piece[:lines], piece[lines:]]
    return dot(jnp.concatenate(parts, axis=1), fz[...])


def plane_back(src, gz, gy, out):
    @pl.loop(0, GROUPS)
    def _(g):
        lhs = src[:, pl.ds(pl.multiple_of(g * GLANES, GLANES), GLANES)].astype(BF)
        u = dot(lhs, gz[...]).astype(BF)
        for q in range(0, OCT, 2):
            cols = []
            for h in range(2):
                o = q + h
                cols.append(
                    jnp.concatenate(
                        [u[:, (2 * o + r) * NZ : (2 * o + r + 1) * NZ] for r in range(2)], axis=0
                    )
                )
            res = dot(gy[...], jnp.concatenate(cols, axis=1))
            out[g * OCT + q] = res[:, :NZ]
            out[g * OCT + q + 1] = res[:, NZ:]


def plain_forward(src, fy, fz, out, lines):
    @pl.loop(0, GROUPS)
    def _(g):
        at = pl.multiple_of(g * GLANES, GLANES)
        out[:, pl.ds(at, GLANES)] = forward_group(src, g, fy, fz, lines)


def load_groups(hbm, buf, sems):
    copies = []
    for g in range(GROUPS):
        part = pl.ds(g * OCT, OCT)
        copies.append(pltpu.make_async_copy(hbm.at[part], buf.at[part], sems.at[g]))
        copies[-1].start()
    return copies


def greet(n):
    me = lax.axis_index("mp")

    @pl.loop(1, n)
    def _(s):
        pl.semaphore_signal(
            pltpu.get_barrier_semaphore(),
            inc=1,
            device_id={"mp": lax.rem(me + s, n)},
            device_id_type=pl.DeviceIdType.MESH,
        )


def remote(src, dst, send, recv, peer):
    return pltpu.make_async_remote_copy(
        src_ref=src,
        dst_ref=dst,
        send_sem=send,
        recv_sem=recv,
        device_id={"mp": peer},
        device_id_type=pl.DeviceIdType.MESH,
    )


def send_half(n, half, src, dst, send, recv, own):
    me = lax.axis_index("mp")
    wide = GLANES * GROUPS // 2
    lanes = pl.ds(half * wide, wide)

    @pl.loop(1, n)
    def _(s):
        peer = lax.rem(me + s, n)
        remote(
            src.at[peer, :, lanes],
            dst.at[me, :, lanes],
            send.at[half, peer],
            recv.at[half, me],
            peer,
        ).start()

    mine = pltpu.make_async_copy(src.at[me, :, lanes], dst.at[me, :, lanes], own.at[half])
    mine.start()
    return mine


def wait_half(n, half, src, dst, send, recv):
    me = lax.axis_index("mp")
    wide = GLANES * GROUPS // 2
    lanes = pl.ds(half * wide, wide)

    @pl.loop(1, n)
    def _(s):
        peer = lax.rem(me + s, n)
        both = remote(
            src.at[peer, :, lanes],
            dst.at[peer, :, lanes],
            send.at[half, peer],
            recv.at[half, peer],
            peer,
        )
        both.wait_recv()
        both.wait_send()


def spread_out(rows, n, field, fy, fz, fx2, spec, src, dst, send, recv, own, ready):
    mine = []
    for half in range(2):
        for g in range(half * GROUPS // 2, (half + 1) * GROUPS // 2):
            ready(g)
            res = forward_group(field, g, fy, fz, KY * rows)
            src[:, :, g * GLANES : (g + 1) * GLANES] = res.reshape(KY, rows, GLANES)
        if half == 0:
            pl.semaphore_wait(pltpu.get_barrier_semaphore(), n - 1)
        mine.append(send_half(n, half, src, dst, send, recv, own))
    each = GLANES // 2
    for half in range(2):
        mine[half].wait()
        wait_half(n, half, src, dst, send, recv)
        for g in range(half * GROUPS // 2, (half + 1) * GROUPS // 2):
            pair = [
                dst[:, :, g * GLANES + r * each : g * GLANES + (r + 1) * each].reshape(NX, each)
                for r in range(2)
            ]
            spec[:, g * each : (g + 1) * each] = jnp.dot(
                fx2[...],
                jnp.concatenate(pair, axis=0),
                precision=precise,
                preferred_element_type=F32,
            )


def analysis_kernel(rows, n, feat_hbm, fy, fz, fx2, spec, feat, load, src, dst, send, recv, own):
    greet(n)
    loads = load_groups(feat_hbm, feat, load)
    spread_out(
        rows, n, feat, fy, fz, fx2, spec, src, dst, send, recv, own, lambda g: loads[g].wait()
    )


def forward_kernel(rows, feat, fy, fz, out):
    plain_forward(feat, fy, fz, out, KY * rows)


TILE = 16
STEP = 4


def tile_of(ref, t):
    at = pl.multiple_of(t * TILE, TILE)
    return ref[:, pl.ds(at, TILE), :].reshape(C * TILE, NZ)


def put_tile(ref, t, value):
    at = pl.multiple_of(t * TILE, TILE)
    ref[:, pl.ds(at, TILE), :] = value.reshape(C, TILE, NZ)


def widen(weight):
    n = C * TILE
    row = lax.broadcasted_iota(jnp.int32, (n, C), 0) // TILE
    up = jnp.where(row == lax.broadcasted_iota(jnp.int32, (n, C), 1), 1.0, 0.0).astype(BF)
    left = dot(up, weight).astype(BF)
    full = lax.dot_general(left, up, (((1,), (1,)), ((), ())), preferred_element_type=F32)
    ri = lax.broadcasted_iota(jnp.int32, (n, n), 0)
    ci = lax.broadcasted_iota(jnp.int32, (n, n), 1)
    return jnp.where(ri % TILE == ci % TILE, full, 0.0).astype(BF)


def middle_kernel(
    rows, n, feat_hbm, cot_hbm, modes, weight, bias, gz, gy, fy, fz, fx2, pg_hbm, part, sums,
    field, acc, bacc, kron, feat, cot, pg, fsem, csem, psem, *net,
):
    if net:
        greet(n)
    loads = load_groups(feat_hbm, feat, fsem) + load_groups(cot_hbm, cot, csem)
    kron[...] = widen(weight[...])
    acc[...] = jnp.zeros_like(acc)
    bacc[...] = jnp.zeros_like(bacc)
    plane_back(modes, gz, gy, field)
    for copy in loads:
        copy.wait()

    @pl.loop(0, rows * NY // (STEP * TILE))
    def _(s):
        f = jnp.concatenate([tile_of(feat, STEP * s + h) for h in range(STEP)], axis=1)
        mix = dot(kron[...], f)
        gs = []
        for h in range(STEP):
            t = STEP * s + h
            x = mix[:, h * NZ : (h + 1) * NZ] + tile_of(field, t) + bias[...]
            x2 = x * x
            a = math.sqrt(2.0 / math.pi)
            th = jnp.tanh(x * (a + (a * 0.044715) * x2))
            d = (0.5 + 0.5 * th) * (1.0 + (x * (1.0 - th)) * (a + (3.0 * a * 0.044715) * x2))
            g = (tile_of(cot, t).astype(F32) * d).astype(BF)
            put_tile(pg, t, g)
            gs.append(g)
        bacc[...] += sum(g.astype(F32) for g in gs)
        g = jnp.concatenate(gs, axis=1)
        acc[...] += lax.dot_general(g, f, (((1,), (1,)), ((), ())), preferred_element_type=F32)

    save = pltpu.make_async_copy(pg, pg_hbm, psem)
    save.start()
    size = C * TILE
    ri = lax.broadcasted_iota(jnp.int32, (size, size), 0)
    ci = lax.broadcasted_iota(jnp.int32, (size, size), 1)
    masked = jnp.where(ri % TILE == ci % TILE, acc[...], 0.0)
    rows_sum = jnp.sum(masked.reshape(C, TILE, size), axis=1)
    fold = jnp.where(
        lax.broadcasted_iota(jnp.int32, (size, LANES), 0) // TILE
        == lax.broadcasted_iota(jnp.int32, (size, LANES), 1),
        1.0,
        0.0,
    ).astype(F32)
    pw = jnp.dot(rows_sum, fold, precision=precise, preferred_element_type=F32)
    by_row = jnp.sum(bacc[...].reshape(C, TILE, NZ), axis=1)
    lane = lax.broadcasted_iota(jnp.int32, (C, LANES), 1)
    sums[...] = pw + jnp.where(lane == C, jnp.sum(by_row, axis=1, keepdims=True), 0.0)
    if net:
        spread_out(rows, n, pg, fy, fz, fx2, part, *net, lambda g: None)
    else:
        plain_forward(pg, fy, fz, part, KY * rows)
    save.wait()


def last_kernel(rows, pg_hbm, modes, weight, gz, gy, out_hbm, field, kron, pg, out, fsem, osem):
    loads = load_groups(pg_hbm, pg, fsem)
    kron[...] = widen(weight[...])
    plane_back(modes, gz, gy, field)
    for copy in loads:
        copy.wait()
    saves = []
    cells = rows * NY // SAVES
    for piece in range(SAVES):

        @pl.loop(0, cells // (STEP * TILE))
        def _(i):
            s = piece * (cells // (STEP * TILE)) + i
            f = jnp.concatenate([tile_of(pg, STEP * s + h) for h in range(STEP)], axis=1)
            mix = dot(kron[...], f)
            for h in range(STEP):
                t = STEP * s + h
                r = mix[:, h * NZ : (h + 1) * NZ] + tile_of(field, t)
                put_tile(out, t, r.astype(BF))

        at = pl.ds(piece * cells, cells)
        saves.append(pltpu.make_async_copy(out.at[:, at], out_hbm.at[:, at], osem.at[piece]))
        saves[-1].start()
    for copy in saves:
        copy.wait()


def exchange_kernel(n, arrays, spread, *refs):
    me = lax.axis_index("mp")
    greet(n)
    srcs = refs[:arrays]
    if spread:
        table, refs, lines = refs[arrays], refs[:arrays] + refs[arrays + 1 : -1], refs[-1]
        each = GLANES // 2
        for g in range(GROUPS):
            part = srcs[0][:, g * each : (g + 1) * each]
            both = jnp.dot(table[...], part, precision=precise, preferred_element_type=F32)
            for r in range(2):
                at = g * GLANES + r * each
                lines[:, :, at : at + each] = both[r * NX : (r + 1) * NX].reshape(n, NX // n, each)
        srcs = (lines, *srcs[1:])
    dsts = refs[arrays : 2 * arrays]
    send, recv, own = refs[2 * arrays :]
    pl.semaphore_wait(pltpu.get_barrier_semaphore(), n - 1)

    @pl.loop(1, n)
    def _(s):
        peer = lax.rem(me + s, n)
        for i in range(arrays):
            remote(
                srcs[i].at[peer], dsts[i].at[me], send.at[i, peer], recv.at[i, me], peer
            ).start()

    for i in range(arrays):
        mine = pltpu.make_async_copy(srcs[i].at[me], dsts[i].at[me], own.at[i])
        mine.start()
        mine.wait()

    @pl.loop(1, n)
    def _(s):
        peer = lax.rem(me + s, n)
        for i in range(arrays):
            both = remote(
                srcs[i].at[peer], dsts[i].at[peer], send.at[i, peer], recv.at[i, peer], peer
            )
            both.wait_recv()
            both.wait_send()


def exchange(xs, n, cid, table=None):
    shapes = [jax.ShapeDtypeStruct(x.shape, x.dtype) for x in xs]
    extra = []
    if table is not None:
        shapes[0] = jax.ShapeDtypeStruct((n, NX // n, 2 * C * KZ), F32)
        extra = [table]
    return pl.pallas_call(
        functools.partial(exchange_kernel, n, len(xs), table is not None),
        out_shape=shapes,
        in_specs=[VMEM] * (len(xs) + len(extra)),
        out_specs=[VMEM] * len(xs),
        scratch_shapes=[
            pltpu.SemaphoreType.DMA((len(xs), n)),
            pltpu.SemaphoreType.DMA((len(xs), n)),
            pltpu.SemaphoreType.DMA((len(xs),)),
        ]
        + [pltpu.VMEM(shapes[0].shape, F32)] * len(extra),
        compiler_params=pltpu.CompilerParams(
            collective_id=cid, has_side_effects=True, vmem_limit_bytes=16 << 20
        ),
        name=f"exchange{cid}",
    )(*xs, *extra)


def call(kernel, rows, outs, scratch, args, name, far=(), far_out=(), cid=None):
    outs = list(outs)
    params = {} if cid is None else {"collective_id": cid, "has_side_effects": True}
    return pl.pallas_call(
        functools.partial(kernel, rows),
        out_shape=outs,
        in_specs=[HBM if i in far else VMEM for i in range(len(args))],
        out_specs=[HBM if i in far_out else VMEM for i in range(len(outs))],
        scratch_shapes=scratch,
        compiler_params=pltpu.CompilerParams(vmem_limit_bytes=60 << 20, **params),
        name=name,
    )(*args)


def owner_blocks(part, n, rows):
    subs = n // KY
    if subs > 1:
        v = part.reshape(KY, rows, 2 * C, subs, KZ // subs)
        part = jnp.transpose(v, (0, 3, 1, 2, 4))
    return part.reshape(n, rows, 2 * C * KZ // subs)


def plane_blocks(got, n, rows):
    subs = n // KY
    if subs > 1:
        v = got.reshape(KY, subs, rows, 2 * C, KZ // subs)
        got = jnp.transpose(v, (0, 2, 3, 1, 4))
    return got.reshape(KY * rows, 2 * C * KZ)


def lines_forward(g, fx):
    g = g.reshape(NX, -1)
    t = jnp.einsum("qx,xl->ql", fx, g, precision=precise).reshape(2, KX, GROUPS, 2, OCT, -1)
    real = t[0, :, :, 0] + t[1, :, :, 1]
    imag = t[0, :, :, 1] - t[1, :, :, 0]
    real, imag = (jnp.transpose(v.reshape(KX, C, -1), (2, 0, 1)) for v in (real, imag))
    return real, imag


def lines_back(real, imag, gx, n, rows):
    u = jnp.stack([real, imag]).reshape(2, real.shape[0], KX, GROUPS, OCT)
    u = jnp.transpose(u, (2, 3, 0, 4, 1)).reshape(KX, -1)
    b = jnp.einsum("qa,al->ql", gx, u, precision=precise).reshape(2, NX, GROUPS, 2, -1)
    lines = jnp.stack([b[0, :, :, 0] - b[1, :, :, 1], b[0, :, :, 1] + b[1, :, :, 0]], 2)
    return lines.reshape(n, rows, -1)


def split_modes(spec):
    v = jnp.transpose(spec.reshape(2, KX, C, KZ), (0, 3, 1, 2))
    return v[0], v[1]


def join_modes(real, imag):
    return jnp.transpose(jnp.stack([real, imag]), (0, 2, 3, 1)).reshape(2 * KX, C * KZ)


def shards(features, cotangent, spectral_weight, pointwise_weight, biases):
    n = lax.axis_size("mp")
    rows = NX // n
    fy, gy, fz, fz_w, gz, gz_w, fx, gx, fx2, gx2 = [jnp.asarray(t) for t in tables(rows)]
    cells = rows * NY
    feat = features.reshape(C, cells, NZ)
    cot = cotangent.reshape(C, cells, NZ)
    bias = jnp.repeat(biases, TILE)[:, None]
    spread = jax.ShapeDtypeStruct((KY * rows, 2 * C * KZ), F32)
    whole = jax.ShapeDtypeStruct((C, cells, NZ), BF)
    field = pltpu.VMEM((C, cells, NZ), F32)
    block = pltpu.VMEM((C, cells, NZ), BF)
    wide = C * TILE
    dma = pltpu.SemaphoreType.DMA
    sems = dma((GROUPS,))
    fused = n == KY
    lines = pltpu.VMEM((n, rows, 2 * C * KZ), F32)
    net = [lines, lines, dma((2, n)), dma((2, n)), dma((2,))] if fused else []
    if fused:
        spread = jax.ShapeDtypeStruct((2 * KX, C * KZ), F32)
        spec = call(
            lambda r, *refs: analysis_kernel(r, n, *refs),
            rows,
            [spread],
            [block, sems, *net],
            (feat, fy, fz, fx2),
            "analysis",
            far=(0,),
            cid=1,
        )[0]
        v_r, v_i = split_modes(spec)
    else:
        part = call(forward_kernel, rows, [spread], [], (feat, fy, fz), "analysis")[0]
        v_r, v_i = lines_forward(exchange([owner_blocks(part, n, rows)], n, 1)[0], fx)
    w_r, w_i = spectral_weight[:, 0], spectral_weight[:, 1]
    s_r, s_i = v_r[..., None], v_i[..., None]
    u_r = jnp.sum(s_r * w_r - s_i * w_i, axis=2)
    u_i = jnp.sum(s_r * w_i + s_i * w_r, axis=2)
    if fused:
        modes = exchange([join_modes(u_r, u_i)], n, 2, gx2)[0]
    else:
        modes = exchange([lines_back(u_r, u_i, gx, n, rows)], n, 2)[0]
    pg, dpart, sums = call(
        lambda r, *refs: middle_kernel(r, n, *refs),
        rows,
        [whole, spread, jax.ShapeDtypeStruct((C, LANES), F32)],
        [
            field,
            pltpu.VMEM((wide, wide), F32),
            pltpu.VMEM((wide, NZ), F32),
            pltpu.VMEM((wide, wide), BF),
            block,
            block,
            block,
            sems,
            sems,
            dma,
            *net,
        ],
        (feat, cot, plane_blocks(modes, n, rows), pointwise_weight, bias, gz_w, gy, fy, fz_w, fx2),
        "middle",
        far=(0, 1),
        far_out=(0,),
        cid=3 if fused else None,
    )
    if fused:
        d_r, d_i = split_modes(dpart)
    else:
        d_r, d_i = lines_forward(exchange([owner_blocks(dpart, n, rows)], n, 3)[0], fx)
    e_r, e_i = d_r[:, :, None, :], d_i[:, :, None, :]
    m_r = jnp.sum(e_r * w_r + e_i * w_i, axis=3)
    m_i = jnp.sum(e_i * w_r - e_r * w_i, axis=3)
    packed = jnp.concatenate(
        [sums[:, :C].reshape(-1, LANES), jnp.pad(sums[:, C], (0, LANES - C))[None]], axis=0
    )
    mine = jnp.broadcast_to(packed, (n, *packed.shape))
    if fused:
        back, every = exchange([join_modes(m_r, m_i), mine], n, 4, gx2)
    else:
        back, every = exchange([lines_back(m_r, m_i, gx, n, rows), mine], n, 4)
    total = jnp.sum(every, axis=0)
    first = jnp.stack([v_r, -v_i], axis=1)[..., None]
    second = jnp.stack([v_i, v_r], axis=1)[..., None]
    spectral_grad = first * e_r[:, None] + second * e_i[:, None]
    grad = call(
        last_kernel,
        rows,
        [whole],
        [field, pltpu.VMEM((wide, wide), BF), block, block, sems, pltpu.SemaphoreType.DMA((SAVES,))],
        (pg, plane_blocks(back, n, rows), pointwise_weight.T, gz, gy),
        "synthesis",
        far=(0,),
        far_out=(0,),
    )[0]
    factor = float(NX * NY * NZ) ** (-0.5)
    total = total * factor
    return (grad.reshape(features.shape), spectral_grad, total[:-1].reshape(C, C), total[-1, :C])


def solution(mesh):
    return jax.shard_map(
        shards,
        mesh=mesh,
        in_specs=(
            P(None, ("groups", "mp"), None, None),
            P(None, ("groups", "mp"), None, None),
            P("mp", None, None, None, None),
            P(),
            P(),
        ),
        out_specs=(
            P(None, ("groups", "mp"), None, None),
            P(("groups", "mp"), None, None, None, None),
            P("groups", None),
            P("groups"),
        ),
        check_vma=False,
    )
```
